32 devices in a mesh: groups: 2 (over y), ckpt: 4 (over z), hid: 4 (over x, core).
Axes of the slice: x: 2, y: 2, z: 4, core: 2. Of those that a mesh axis runs over, the one named last changes fastest.
Arguments:
- residual_stream: bfloat16 [4, 768, 2048], P('ckpt', ('groups', 'hid')), parts along dimension 1, may hold values from -6 to 6
- norm_gain: float32 [4, 2048], P('ckpt'), may hold values from 0.1 to 1.9
- norm_shift: float32 [4, 2048], P('ckpt'), may hold values from -3 to 3
- input_weight: bfloat16 [4, 2048, 4096], P('ckpt', None, 'hid'), may hold values from -0.125 to 0.125
- input_bias: float32 [4, 4096], P('ckpt', 'hid'), may hold values from -3 to 3
- output_weight: bfloat16 [4, 4096, 2048], P('ckpt', 'hid'), may hold values from -0.09375 to 0.09375
- output_bias: float32 [4, 2048], P('ckpt'), may hold values from -3 to 3
- encoder_weight: bfloat16 [4, 2048, 4096], P('ckpt', None, 'hid'), may hold values from -0.0625 to 0.0625
- encoder_bias: float32 [4096], P('hid'), may hold values from -3 to 3
- decoder_weight: bfloat16 [4, 4096, 2048], P('ckpt', None, 'hid'), may hold values from -0.09375 to 0.09375
- decoder_bias: float32 [4, 2048], P('ckpt', 'hid'), may hold values from -3 to 3
Outputs:
- latent_codes: bfloat16 [768, 4096], P('groups', 'hid'), parts along dimension 0
- recon_error: float32 [4, 768, 2048], P('ckpt', 'groups', 'hid'), parts along dimension 1
The draws below stay inside these ranges and needn't reach their ends.
There are 2 independent parts, one for each index of `groups`. The reference program is written for one: setup_inputs(seed, part) draws one part's arguments, and reference() takes and returns one part's arrays. A program takes and returns all parts, laid end to end along the dimension named above; an argument that names none is the same for every part. Nothing has to cross between parts.
All inputs are finite; a program needn't handle non-finite values.
Results may differ from the reference program's by a relative error of at most 0.0056.
Values may be sent and summed in bfloat16 or wider, within the bound.
A program may use at most 64 MiB of HBM per device.

```python
import jax
import jax.numpy as jnp
from jax import lax

D = 2048
FF = 4096
LAT = 4096
ROWS = 384
CKPT = 4


def steps_of(rng, dims, split, low, largest):
    gain = 1.0
    for position, shards_of in split:
        steps = jax.random.uniform(jax.random.fold_in(jax.random.fold_in(rng, 6), position), (shards_of,), jnp.float32, low / len(split), largest / len(split))
        gain = gain * jnp.repeat(jnp.exp(steps), dims[position] // shards_of).reshape((-1,) + (1,) * (len(dims) - 1 - position))
    return gain


def bell_draw(own_key, shape, spread, bound, shards=(), kind=jnp.bfloat16):
    level = steps_of(own_key, shape, shards, -0.22, 0.18) if shards else 1.0
    array = jax.random.normal(own_key, shape, jnp.float32) * spread * level
    return jnp.minimum(jnp.maximum(array, -bound), bound).astype(kind)


def setup_inputs(seed: int = 0, part: int = 0) -> dict:
    key_list = jax.random.split(jax.random.key(seed), 12)
    part_splits = jax.random.split(jax.random.fold_in(key_list[11], part), 12)
    residual_stream = bell_draw(part_splits[0], (CKPT, ROWS, D), 1.0, 6.0, ((0, 4), (1, 4)))
    norm_gain = jnp.clip(1.0 + 0.18 * jax.random.normal(key_list[1], (CKPT, D), jnp.float32), 0.1, 1.9)
    norm_shift = bell_draw(key_list[2], (CKPT, D), 0.5, 3.0, ((0, 4),), jnp.float32)
    input_weight = bell_draw(key_list[3], (CKPT, D, FF), D ** -0.5, 0.125, ((0, 4), (2, 4)))
    input_bias = bell_draw(key_list[4], (CKPT, FF), 0.5, 3.0, ((0, 4), (1, 4)), jnp.float32)
    output_weight = bell_draw(key_list[5], (CKPT, FF, D), FF ** -0.5, 0.09375, ((0, 4), (1, 4)))
    output_bias = bell_draw(key_list[6], (CKPT, D), 0.5, 3.0, ((0, 4),), jnp.float32)
    encoder_weight = bell_draw(key_list[7], (CKPT, D, LAT), (D * CKPT) ** -0.5, 0.0625, ((0, 4), (2, 4)))
    encoder_bias = bell_draw(key_list[8], (LAT,), 0.5, 3.0, ((0, 4),), jnp.float32)
    decoder_weight = bell_draw(key_list[9], (CKPT, LAT, D), LAT ** -0.5, 0.09375, ((0, 4), (2, 4)))
    decoder_bias = bell_draw(key_list[10], (CKPT, D), 0.5, 3.0, ((0, 4), (1, 4)), jnp.float32)
    return dict(residual_stream=residual_stream, norm_gain=norm_gain, norm_shift=norm_shift, input_weight=input_weight, input_bias=input_bias, output_weight=output_weight, output_bias=output_bias, encoder_weight=encoder_weight, encoder_bias=encoder_bias, decoder_weight=decoder_weight, decoder_bias=decoder_bias)


def normalize(stream, gain_row, shift_row):
    values = stream.astype(jnp.float32)
    average = lax.optimization_barrier(jnp.mean(values, axis=-1, keepdims=True))
    centred = values - average
    variance = lax.optimization_barrier(jnp.mean(centred * centred, axis=-1, keepdims=True))
    return centred * lax.rsqrt(variance + 1e-05) * gain_row + shift_row

def reference(residual_stream, norm_gain, norm_shift, input_weight, input_bias, output_weight, output_bias, encoder_weight, encoder_bias, decoder_weight, decoder_bias):

    def one_model(operands):
        stream, gain_row, shift_row, first_weight, first_bias, second_weight, second_bias = operands
        normed = normalize(stream, gain_row, shift_row).astype(jnp.bfloat16)
        hidden = jax.nn.gelu(jnp.dot(normed, first_weight, preferred_element_type=jnp.float32) + first_bias, approximate=False).astype(jnp.bfloat16)
        return (jnp.dot(hidden, second_weight, preferred_element_type=jnp.float32) + second_bias).astype(jnp.bfloat16)
    mlp_out = lax.map(one_model, (residual_stream, norm_gain, norm_shift, input_weight, input_bias, output_weight, output_bias))

    def accumulate(running, operands):
        return (running + jnp.dot(operands[0], operands[1], preferred_element_type=jnp.float32), None)
    pre_codes, _ = lax.scan(accumulate, jnp.zeros((ROWS, LAT), jnp.float32), (mlp_out, encoder_weight))
    latent_codes = jax.nn.relu(pre_codes + encoder_bias).astype(jnp.bfloat16)

    def decode(operands):
        outputs, weights, biases = operands
        return outputs.astype(jnp.float32) - (jnp.dot(latent_codes, weights, preferred_element_type=jnp.float32) + biases)
    recon_error = lax.map(decode, (mlp_out, decoder_weight, decoder_bias))
    return (latent_codes, recon_error)
```

```python
import functools

import jax
import jax.numpy as jnp
from jax import lax
from jax.experimental import pallas as pl
from jax.experimental.pallas import tpu as pltpu
from jax.sharding import PartitionSpec as P


def with_collectives(
    residual_stream,
    norm_gain,
    norm_shift,
    input_weight,
    input_bias,
    output_weight,
    output_bias,
    encoder_weight,
    encoder_bias,
    decoder_weight,
    decoder_bias,
):
    values = residual_stream[0].astype(jnp.float32)
    average = jnp.mean(values, axis=-1, keepdims=True)
    centred = values - average
    variance = jnp.mean(centred * centred, axis=-1, keepdims=True)
    normed = (centred * lax.rsqrt(variance + 1e-05) * norm_gain[0] + norm_shift[0]).astype(
        jnp.bfloat16
    )
    first_weight = input_weight[0]
    first_bias = input_bias[0]
    second_weight = output_weight[0]
    hidden = jax.nn.gelu(
        jnp.dot(
            lax.all_gather(normed, "hid", axis=0, tiled=True),
            first_weight,
            preferred_element_type=jnp.float32,
        )
        + first_bias,
        approximate=False,
    ).astype(jnp.bfloat16)
    partial_out = jnp.dot(hidden, second_weight, preferred_element_type=jnp.float32)
    mlp_out = (lax.psum(partial_out, "hid") + output_bias[0]).astype(jnp.bfloat16)
    encoder_terms = jnp.dot(mlp_out, encoder_weight[0], preferred_element_type=jnp.float32)
    latent_codes = jax.nn.relu(lax.psum(encoder_terms, "ckpt") + encoder_bias).astype(jnp.bfloat16)
    local_decoder = decoder_weight[0]
    column_count = local_decoder.shape[1]
    rebuilt = (
        jnp.dot(
            lax.all_gather(latent_codes, "hid", axis=1, tiled=True),
            local_decoder,
            preferred_element_type=jnp.float32,
        )
        + decoder_bias[0]
    )
    own_columns = lax.dynamic_slice_in_dim(
        mlp_out, lax.axis_index("hid") * column_count, column_count, 1
    ).astype(jnp.float32)
    recon_error = (own_columns - rebuilt)[None]
    return (latent_codes, recon_error)


CHUNKS = 2
F32, BF16 = jnp.float32, jnp.bfloat16


def kernel(
    n, res, gain, shift, b1, b2, be, bd, w1_hbm, w2_hbm, we_hbm, wd_hbm, codes_out, recon_out,
    w1, w2, we, wd, nbuf, hbuf, psend, precv, pown, xsend, xrecv, mbuf, pre, zsend, zrecv, cbuf, obuf,
    sw, sa, ra, sb, rb, sx, rx, sm, rm, sz, rz, sc, rc, sd, rd, se, re, so,
):
    K = CHUNKS
    S = nbuf.shape[2]
    M = n * S
    D = nbuf.shape[3]
    FFL = w1.shape[1]
    LATL = we.shape[1]
    TW = D // n
    T = n // 2
    NX = n // 2
    NZ = n
    h = lax.axis_index("hid")
    z = lax.axis_index("ckpt")
    c = lax.rem(h, 2)
    sib = h + 1 - 2 * c
    sends = []

    def hpeer(j):
        return lax.rem(h + 2 * j, n)

    def hfrom(j):
        return lax.rem(h + n - 2 * j, n)

    def zpeer(j):
        return lax.rem(z + j, NZ)

    def zfrom(j):
        return lax.rem(z + NZ - j, NZ)

    def remote(src, dst, ssem, rsem, **dev):
        return pltpu.make_async_remote_copy(
            src_ref=src, dst_ref=dst, send_sem=ssem, recv_sem=rsem,
            device_id=dev, device_id_type=pl.DeviceIdType.MESH,
        )

    def send(src, dst, ssem, rsem, **dev):
        copy = remote(src, dst, ssem, rsem, **dev)
        copy.start()
        sends.append(copy)

    def arrived(dst, ssem, rsem):
        remote(dst, dst, ssem, rsem, hid=sib).wait_recv()

    loads = [
        pltpu.make_async_copy(a, b, sw.at[i])
        for i, (a, b) in enumerate(((w1_hbm, w1), (w2_hbm, w2), (we_hbm, we), (wd_hbm, wd)))
    ]
    for load in loads:
        load.start()

    barrier = pltpu.get_barrier_semaphore()
    peers = [dict(hid=sib)] + [dict(hid=hpeer(j)) for j in range(1, NX)]
    peers += [dict(ckpt=zpeer(j)) for j in range(1, NZ)]
    for dev in peers:
        pl.semaphore_signal(barrier, inc=1, device_id=dev, device_id_type=pl.DeviceIdType.MESH)

    def normalise(k):
        values = res[k * S : (k + 1) * S, :].astype(F32)
        average = jnp.mean(values, axis=-1, keepdims=True)
        centred = values - average
        variance = jnp.mean(centred * centred, axis=-1, keepdims=True)
        nbuf[k, h] = (centred * lax.rsqrt(variance + 1e-05) * gain[...] + shift[...]).astype(BF16)

    def spread(k):
        for j in range(1, NX):
            send(nbuf.at[k, h], nbuf.at[k, h], sa.at[k, 1, j], ra.at[k, h], hid=hpeer(j))
        send(nbuf.at[k, h], nbuf.at[k, h], sa.at[k, 0, 0], ra.at[k, h], hid=sib)

    def relay(k):
        for j in range(1, NX):
            o = hfrom(j)
            arrived(nbuf.at[k, o], sa.at[k, 0, 0], ra.at[k, o])
            send(nbuf.at[k, o], nbuf.at[k, o], sa.at[k, 0, j], ra.at[k, o], hid=sib)

    def first(k):
        arrived(nbuf.at[k, sib], sa.at[k, 0, 0], ra.at[k, sib])
        for j in range(1, NX):
            o = lax.rem(sib + n - 2 * j, n)
            arrived(nbuf.at[k, o], sa.at[k, 0, 0], ra.at[k, o])
        if k == 0:
            loads[0].wait()

        def tile(i, _):
            cols = pl.ds(pl.multiple_of(i * 256, 256), 256)
            u = jnp.dot(nbuf[k].reshape(M, D), w1[:, cols], preferred_element_type=F32) + b1[:, cols]
            hbuf[:, cols] = (0.5 * u * (1.0 + lax.erf(u * 0.7071067811865476))).astype(BF16)
            return 0

        lax.fori_loop(0, FFL // 256, tile, 0)

    def project(g):
        cols = pl.ds(pl.multiple_of(g * TW, TW), TW)
        return jnp.dot(hbuf[...], w2[:, cols], preferred_element_type=F32)

    def second(k, between):
        if k == 0:
            loads[1].wait()
        for t in range(T):
            psend[k, t] = project((1 - c) * T + t).astype(BF16)
            send(psend.at[k, t], precv.at[k, t], sb.at[k, t], rb.at[k, t], hid=sib)
        between()
        for t in range(T):
            own = project(c * T + t)
            arrived(precv.at[k, t], sb.at[k, t], rb.at[k, t])
            own = own + precv[k, t].astype(F32)
            pown[k, t] = own
            xsend[k, t] = own.astype(BF16)
            for j in range(1, NX):
                send(xsend.at[k, t], xrecv.at[k, t, j], sx.at[k, t, j], rx.at[k, t, j], hid=hpeer(j))

    def encode(k, g, start):
        rows = pl.ds(pl.multiple_of(g * TW, TW), TW)

        def tile(i, _):
            cols = pl.ds(pl.multiple_of(i * 256, 256), 256)
            u = jnp.dot(mbuf[k, g], we[rows, cols], preferred_element_type=F32)
            pre[k, :, cols] = u if start else pre[k, :, cols] + u
            return 0

        lax.fori_loop(0, LATL // 256, tile, 0)

    def finish(k):
        for t in range(T):
            g = c * T + t
            total = pown[k, t]
            for j in range(1, NX):
                arrived(xrecv.at[k, t, j], sx.at[k, t, j], rx.at[k, t, j])
                total = total + xrecv[k, t, j].astype(F32)
            mbuf[k, g] = (total + b2[:, pl.ds(pl.multiple_of(g * TW, TW), TW)]).astype(BF16)
            send(mbuf.at[k, g], mbuf.at[k, g], sm.at[k, t], rm.at[k, t], hid=sib)
            if k == 0 and t == 0:
                loads[2].wait()
            encode(k, g, t == 0)
        for t in range(T):
            g = (1 - c) * T + t
            arrived(mbuf.at[k, g], sm.at[k, t], rm.at[k, t])
            encode(k, g, False)
        for j in range(1, NZ):
            b = zpeer(j)
            zsend[k, j] = pre[k, pl.ds(pl.multiple_of(b * S, S), S), :].astype(BF16)
            send(zsend.at[k, j], zrecv.at[k, j], sz.at[k, j], rz.at[k, j], ckpt=b)

    def codes(k):
        total = pre[k, pl.ds(pl.multiple_of(z * S, S), S), :]
        for j in range(1, NZ):
            arrived(zrecv.at[k, j], sz.at[k, j], rz.at[k, j])
            total = total + zrecv[k, j].astype(F32)
        cbuf[k, h, z] = jnp.maximum(total + be[...], 0.0).astype(BF16)
        for j in range(1, NZ):
            send(cbuf.at[k, h, z], cbuf.at[k, h, z], sc.at[k, j], rc.at[k, j], ckpt=zpeer(j))
        across(k, 0)

    def across(k, i):
        b = zfrom(i)
        for j in range(1, NX):
            send(cbuf.at[k, h, b], cbuf.at[k, h, b], sd.at[k, i, j], rd.at[k, b, j], hid=hpeer(j))

    outs = []

    def put(src, dst, sem):
        copy = pltpu.make_async_copy(src, dst, sem)
        copy.start()
        outs.append(copy)

    def collect(k):
        for i in range(1, NZ):
            b = zfrom(i)
            arrived(cbuf.at[k, h, b], sc.at[k, i], rc.at[k, i])
            across(k, i)
        send(cbuf.at[k, h], cbuf.at[k, h], se.at[k, 0], re.at[k, 0], hid=sib)
        for b in range(NZ):
            put(cbuf.at[k, h, b], codes_out.at[pl.ds((b * K + k) * S, S), :], so.at[0, k, b])

    def decode(k):
        def part(o):
            return jnp.dot(
                cbuf[k, o].reshape(M, LATL),
                wd[pl.ds(pl.multiple_of(o * LATL, LATL), LATL), :],
                preferred_element_type=F32,
            )

        if k == 0:
            loads[3].wait()
        obuf[k] = mbuf[k, h].astype(F32) - (part(h) + bd[...])
        arrived(cbuf.at[k, sib], se.at[k, 0], re.at[k, 0])
        obuf[k] -= part(sib)
        for j in range(1, NX):
            o = hfrom(j)
            for b in range(NZ):
                arrived(cbuf.at[k, o, b], sd.at[k, b, j], rd.at[k, b, j])
            send(cbuf.at[k, o], cbuf.at[k, o], se.at[k, j], re.at[k, j], hid=sib)
            obuf[k] -= part(o)
        for j in range(1, NX):
            o = lax.rem(sib + n - 2 * j, n)
            arrived(cbuf.at[k, o], se.at[k, j], re.at[k, j])
            obuf[k] -= part(o)
        for b in range(NZ):
            put(obuf.at[k, pl.ds(b * S, S), :], recon_out.at[pl.ds((b * K + k) * S, S), :], so.at[1, k, b])

    normalise(0)
    pl.semaphore_wait(barrier, len(peers))
    spread(0)
    for k in range(1, K):
        normalise(k)
        spread(k)
    relay(0)
    for k in range(K):
        first(k)
        second(k, functools.partial(relay, k + 1) if k + 1 < K else (lambda: None))
    for k in range(K):
        finish(k)
    for k in range(K):
        codes(k)
        collect(k)
    for k in range(K):
        decode(k)
    for copy in outs:
        copy.wait()
    for copy in sends:
        copy.wait_send()


def fused(res, gain, shift, w1, b1, w2, b2, we, be, wd, bd, hid):
    K, n = CHUNKS, hid
    rows, D = res.shape[1:]
    FFL, LATL, OUTL = w1.shape[2], we.shape[2], wd.shape[2]
    S = rows // K
    M = n * S
    T = NX = n // 2
    TW = D // n
    dma = pltpu.SemaphoreType.DMA
    vmem = pl.BlockSpec(memory_space=pltpu.VMEM)
    hbm = pl.BlockSpec(memory_space=pl.ANY)
    codes, recon = pl.pallas_call(
        functools.partial(kernel, n),
        out_shape=(
            jax.ShapeDtypeStruct((n * rows, LATL), BF16),
            jax.ShapeDtypeStruct((n * rows, OUTL), F32),
        ),
        in_specs=[vmem] * 7 + [hbm] * 4,
        out_specs=(hbm, hbm),
        scratch_shapes=[
            pltpu.VMEM(w1.shape[1:], BF16),
            pltpu.VMEM(w2.shape[1:], BF16),
            pltpu.VMEM(we.shape[1:], BF16),
            pltpu.VMEM(wd.shape[1:], BF16),
            pltpu.VMEM((K, n, S, D), BF16),
            pltpu.VMEM((M, FFL), BF16),
            pltpu.VMEM((K, T, M, TW), BF16),
            pltpu.VMEM((K, T, M, TW), BF16),
            pltpu.VMEM((K, T, M, TW), F32),
            pltpu.VMEM((K, T, M, TW), BF16),
            pltpu.VMEM((K, T, NX, M, TW), BF16),
            pltpu.VMEM((K, n, M, TW), BF16),
            pltpu.VMEM((K, M, LATL), F32),
            pltpu.VMEM((K, n, S, LATL), BF16),
            pltpu.VMEM((K, n, S, LATL), BF16),
            pltpu.VMEM((K, n, n, S, LATL), BF16),
            pltpu.VMEM((K, M, OUTL), F32),
            dma((4,)),
            dma((K, 2, NX)),
            dma((K, n)),
            dma((K, T)),
            dma((K, T)),
            dma((K, T, NX)),
            dma((K, T, NX)),
            dma((K, T)),
            dma((K, T)),
            dma((K, n)),
            dma((K, n)),
            dma((K, n)),
            dma((K, n)),
            dma((K, n, NX)),
            dma((K, n, NX)),
            dma((K, NX)),
            dma((K, NX)),
            dma((2, K, n)),
        ],
        compiler_params=pltpu.CompilerParams(
            collective_id=0, has_side_effects=True, vmem_limit_bytes=56 * 1024 * 1024
        ),
    )(
        res[0], gain, shift, b1, b2, be.reshape(1, LATL), bd,
        w1[0], w2[0], we[0], wd[0],
    )
    return codes, recon[None]


def solution(mesh):
    hid, ckpt = mesh.shape["hid"], mesh.shape["ckpt"]

    def body(*operands):
        rows, width = operands[0].shape[1:]
        latents = operands[7].shape[2]
        fits = hid == ckpt and hid % 2 == 0 and rows % (16 * CHUNKS) == 0
        fits = fits and latents % 256 == 0 and width % (256 * hid) == 0
        return (fused if fits and hid <= 4 else with_collectives)(*operands, **(dict(hid=hid) if fits and hid <= 4 else {}))

    placed = (
        P("ckpt", ("groups", "hid"), None),
        P("ckpt", None),
        P("ckpt", None),
        P("ckpt", None, "hid"),
        P("ckpt", "hid"),
        P("ckpt", "hid", None),
        P("ckpt", None),
        P("ckpt", None, "hid"),
        P("hid"),
        P("ckpt", None, "hid"),
        P("ckpt", "hid"),
    )
    return jax.shard_map(
        body,
        mesh=mesh,
        in_specs=placed,
        out_specs=(P("groups", "hid"), P("ckpt", "groups", "hid")),
        check_vma=False,
    )
```

```python
import functools

import jax
import jax.numpy as jnp
from jax import lax
from jax.experimental import pallas as pl
from jax.experimental.pallas import tpu as pltpu
from jax.sharding import PartitionSpec as P


def with_collectives(
    residual_stream,
    norm_gain,
    norm_shift,
    input_weight,
    input_bias,
    output_weight,
    output_bias,
    encoder_weight,
    encoder_bias,
    decoder_weight,
    decoder_bias,
):
    values = residual_stream[0].astype(jnp.float32)
    average = jnp.mean(values, axis=-1, keepdims=True)
    centred = values - average
    variance = jnp.mean(centred * centred, axis=-1, keepdims=True)
    normed = (centred * lax.rsqrt(variance + 1e-05) * norm_gain[0] + norm_shift[0]).astype(
        jnp.bfloat16
    )
    first_weight = input_weight[0]
    first_bias = input_bias[0]
    second_weight = output_weight[0]
    hidden = jax.nn.gelu(
        jnp.dot(
            lax.all_gather(normed, "hid", axis=0, tiled=True),
            first_weight,
            preferred_element_type=jnp.float32,
        )
        + first_bias,
        approximate=False,
    ).astype(jnp.bfloat16)
    partial_out = jnp.dot(hidden, second_weight, preferred_element_type=jnp.float32)
    mlp_out = (lax.psum(partial_out, "hid") + output_bias[0]).astype(jnp.bfloat16)
    encoder_terms = jnp.dot(mlp_out, encoder_weight[0], preferred_element_type=jnp.float32)
    latent_codes = jax.nn.relu(lax.psum(encoder_terms, "ckpt") + encoder_bias).astype(jnp.bfloat16)
    local_decoder = decoder_weight[0]
    column_count = local_decoder.shape[1]
    rebuilt = (
        jnp.dot(
            lax.all_gather(latent_codes, "hid", axis=1, tiled=True),
            local_decoder,
            preferred_element_type=jnp.float32,
        )
        + decoder_bias[0]
    )
    own_columns = lax.dynamic_slice_in_dim(
        mlp_out, lax.axis_index("hid") * column_count, column_count, 1
    ).astype(jnp.float32)
    recon_error = (own_columns - rebuilt)[None]
    return (latent_codes, recon_error)


CHUNKS = 3
F32, BF16 = jnp.float32, jnp.bfloat16


def kernel(
    n, res, gain, shift, b1, b2, be, bd, w1_hbm, w2_hbm, we_hbm, wd_hbm, codes_out, recon_out,
    w1, w2, we, wd, nbuf, hbuf, psend, precv, pown, xsend, xrecv, mbuf, pre, zsend, zrecv, cbuf, obuf,
    sw, sa, ra, sb, rb, sx, rx, sm, rm, sz, rz, sc, rc, sd, rd, se, re, so,
):
    K = CHUNKS
    S = nbuf.shape[2]
    M = n * S
    D = nbuf.shape[3]
    FFL = w1.shape[1]
    LATL = we.shape[1]
    TW = D // n
    T = n // 2
    NX = n // 2
    NZ = n
    h = lax.axis_index("hid")
    z = lax.axis_index("ckpt")
    c = lax.rem(h, 2)
    sib = h + 1 - 2 * c
    sends = []

    def hpeer(j):
        return lax.rem(h + 2 * j, n)

    def hfrom(j):
        return lax.rem(h + n - 2 * j, n)

    def zpeer(j):
        return lax.rem(z + j, NZ)

    def zfrom(j):
        return lax.rem(z + NZ - j, NZ)

    def remote(src, dst, ssem, rsem, **dev):
        return pltpu.make_async_remote_copy(
            src_ref=src, dst_ref=dst, send_sem=ssem, recv_sem=rsem,
            device_id=dev, device_id_type=pl.DeviceIdType.MESH,
        )

    def send(src, dst, ssem, rsem, **dev):
        copy = remote(src, dst, ssem, rsem, **dev)
        copy.start()
        sends.append(copy)

    def arrived(dst, ssem, rsem):
        remote(dst, dst, ssem, rsem, hid=sib).wait_recv()

    loads = [
        pltpu.make_async_copy(a, b, sw.at[i])
        for i, (a, b) in enumerate(((w1_hbm, w1), (w2_hbm, w2), (we_hbm, we), (wd_hbm, wd)))
    ]
    for load in loads:
        load.start()

    barrier = pltpu.get_barrier_semaphore()
    peers = [dict(hid=sib)] + [dict(hid=hpeer(j)) for j in range(1, NX)]
    peers += [dict(ckpt=zpeer(j)) for j in range(1, NZ)]
    for dev in peers:
        pl.semaphore_signal(barrier, inc=1, device_id=dev, device_id_type=pl.DeviceIdType.MESH)

    def normalise(k):
        values = res[k * S : (k + 1) * S, :].astype(F32)
        average = jnp.mean(values, axis=-1, keepdims=True)
        centred = values - average
        variance = jnp.mean(centred * centred, axis=-1, keepdims=True)
        nbuf[k, h] = (centred * lax.rsqrt(variance + 1e-05) * gain[...] + shift[...]).astype(BF16)

    def spread(k):
        for j in range(1, NX):
            send(nbuf.at[k, h], nbuf.at[k, h], sa.at[k, 1, j], ra.at[k, h], hid=hpeer(j))
        send(nbuf.at[k, h], nbuf.at[k, h], sa.at[k, 0, 0], ra.at[k, h], hid=sib)

    def relay(k):
        for j in range(1, NX):
            o = hfrom(j)
            arrived(nbuf.at[k, o], sa.at[k, 0, 0], ra.at[k, o])
            send(nbuf.at[k, o], nbuf.at[k, o], sa.at[k, 0, j], ra.at[k, o], hid=sib)

    def first(k):
        arrived(nbuf.at[k, sib], sa.at[k, 0, 0], ra.at[k, sib])
        for j in range(1, NX):
            o = lax.rem(sib + n - 2 * j, n)
            arrived(nbuf.at[k, o], sa.at[k, 0, 0], ra.at[k, o])
        if k == 0:
            loads[0].wait()

        def tile(i, _):
            cols = pl.ds(pl.multiple_of(i * 256, 256), 256)
            u = jnp.dot(nbuf[k].reshape(M, D), w1[:, cols], preferred_element_type=F32) + b1[:, cols]
            hbuf[:, cols] = (0.5 * u * (1.0 + lax.erf(u * 0.7071067811865476))).astype(BF16)
            return 0

        lax.fori_loop(0, FFL // 256, tile, 0)

    def project(g):
        cols = pl.ds(pl.multiple_of(g * TW, TW), TW)
        return jnp.dot(hbuf[...], w2[:, cols], preferred_element_type=F32)

    def second(k, between):
        if k == 0:
            loads[1].wait()
        for t in range(T):
            psend[k, t] = project((1 - c) * T + t).astype(BF16)
            send(psend.at[k, t], precv.at[k, t], sb.at[k, t], rb.at[k, t], hid=sib)
        between()
        for t in range(T):
            own = project(c * T + t)
            arrived(precv.at[k, t], sb.at[k, t], rb.at[k, t])
            own = own + precv[k, t].astype(F32)
            pown[k, t] = own
            xsend[k, t] = own.astype(BF16)
            for j in range(1, NX):
                send(xsend.at[k, t], xrecv.at[k, t, j], sx.at[k, t, j], rx.at[k, t, j], hid=hpeer(j))

    def encode(k, g, start):
        rows = pl.ds(pl.multiple_of(g * TW, TW), TW)

        def tile(i, _):
            cols = pl.ds(pl.multiple_of(i * 256, 256), 256)
            u = jnp.dot(mbuf[k, g], we[rows, cols], preferred_element_type=F32)
            pre[k, :, cols] = u if start else pre[k, :, cols] + u
            return 0

        lax.fori_loop(0, LATL // 256, tile, 0)

    def finish(k):
        for t in range(T):
            g = c * T + t
            total = pown[k, t]
            for j in range(1, NX):
                arrived(xrecv.at[k, t, j], sx.at[k, t, j], rx.at[k, t, j])
                total = total + xrecv[k, t, j].astype(F32)
            mbuf[k, g] = (total + b2[:, pl.ds(pl.multiple_of(g * TW, TW), TW)]).astype(BF16)
            send(mbuf.at[k, g], mbuf.at[k, g], sm.at[k, t], rm.at[k, t], hid=sib)
            if k == 0 and t == 0:
                loads[2].wait()
            encode(k, g, t == 0)
        for t in range(T):
            g = (1 - c) * T + t
            arrived(mbuf.at[k, g], sm.at[k, t], rm.at[k, t])
            encode(k, g, False)
        for j in range(1, NZ):
            b = zpeer(j)
            zsend[k, j] = pre[k, pl.ds(pl.multiple_of(b * S, S), S), :].astype(BF16)
            send(zsend.at[k, j], zrecv.at[k, j], sz.at[k, j], rz.at[k, j], ckpt=b)

    def codes(k):
        total = pre[k, pl.ds(pl.multiple_of(z * S, S), S), :]
        for j in range(1, NZ):
            arrived(zrecv.at[k, j], sz.at[k, j], rz.at[k, j])
            total = total + zrecv[k, j].astype(F32)
        cbuf[k, h, z] = jnp.maximum(total + be[...], 0.0).astype(BF16)
        pl.when(z < NZ - 1)(passing(k, z, 1).start)
        pl.when(z > 0)(passing(k, z, 0).start)
        over(k, z)

    def passing(k, b, up):
        there = jnp.minimum(z + 1, NZ - 1) if up else jnp.maximum(z - 1, 0)
        block = cbuf.at[k, h, b]
        return remote(block, block, sc.at[k, up, b], rc.at[k, b], ckpt=there)

    def over(k, b):
        for j in range(1, NX):
            crossing(k, b, j).start()

    def crossing(k, b, j):
        block = cbuf.at[k, h, b]
        return remote(block, block, sd.at[k, b, j], rd.at[k, b, j], hid=hpeer(j))

    def passed():
        for k in range(K):
            for b in range(NZ):
                pl.when(jnp.logical_and(b <= z, z < NZ - 1))(passing(k, b, 1).wait_send)
                pl.when(jnp.logical_and(b >= z, z > 0))(passing(k, b, 0).wait_send)
                for j in range(1, NX):
                    crossing(k, b, j).wait_send()

    outs = []

    def put(src, dst, sem):
        copy = pltpu.make_async_copy(src, dst, sem)
        copy.start()
        outs.append(copy)

    def collect(k):
        for i in range(1, NZ):
            @pl.when(z - i >= 0)
            def _():
                b = z - i
                arrived(cbuf.at[k, h, b], sc.at[k, 0, b], rc.at[k, b])
                pl.when(z < NZ - 1)(passing(k, b, 1).start)
                over(k, b)

            @pl.when(z + i < NZ)
            def _():
                b = z + i
                arrived(cbuf.at[k, h, b], sc.at[k, 0, b], rc.at[k, b])
                pl.when(z > 0)(passing(k, b, 0).start)
                over(k, b)

        send(cbuf.at[k, h], cbuf.at[k, h], se.at[k, 0], re.at[k, 0], hid=sib)
        for b in range(NZ):
            put(cbuf.at[k, h, b], codes_out.at[pl.ds((b * K + k) * S, S), :], so.at[0, k, b])

    def decode(k):
        def part(o):
            return jnp.dot(
                cbuf[k, o].reshape(M, LATL),
                wd[pl.ds(pl.multiple_of(o * LATL, LATL), LATL), :],
                preferred_element_type=F32,
            )

        if k == 0:
            loads[3].wait()
        obuf[k] = mbuf[k, h].astype(F32) - (part(h) + bd[...])
        arrived(cbuf.at[k, sib], se.at[k, 0], re.at[k, 0])
        obuf[k] -= part(sib)
        for j in range(1, NX):
            o = hfrom(j)
            for b in range(NZ):
                arrived(cbuf.at[k, o, b], sd.at[k, b, j], rd.at[k, b, j])
            send(cbuf.at[k, o], cbuf.at[k, o], se.at[k, j], re.at[k, j], hid=sib)
            obuf[k] -= part(o)
        for j in range(1, NX):
            o = lax.rem(sib + n - 2 * j, n)
            arrived(cbuf.at[k, o], se.at[k, j], re.at[k, j])
            obuf[k] -= part(o)
        for b in range(NZ):
            put(obuf.at[k, pl.ds(b * S, S), :], recon_out.at[pl.ds((b * K + k) * S, S), :], so.at[1, k, b])

    normalise(0)
    pl.semaphore_wait(barrier, len(peers))
    spread(0)
    for k in range(1, K):
        normalise(k)
        spread(k)
    def mlp(k):
        first(k)
        second(k, functools.partial(relay, k + 1) if k + 1 < K else (lambda: None))

    relay(0)
    mlp(0)
    mlp(1)
    finish(0)
    mlp(2)
    finish(1)
    codes(0)
    finish(2)
    codes(1)
    collect(0)
    codes(2)
    collect(1)
    decode(0)
    collect(2)
    decode(1)
    decode(2)
    for copy in outs:
        copy.wait()
    for copy in sends:
        copy.wait_send()
    passed()


def landing(codes, recon, codes_out, recon_out):
    codes_out[...] = codes[...]
    recon_out[...] = recon[...]


def land(codes, recon):
    vmem = pl.BlockSpec(memory_space=pltpu.VMEM)
    return pl.pallas_call(
        landing,
        out_shape=(
            jax.ShapeDtypeStruct(codes.shape, codes.dtype),
            jax.ShapeDtypeStruct(recon.shape, recon.dtype),
        ),
        in_specs=[vmem] * 2,
        out_specs=(vmem, vmem),
    )(codes, recon)


def fused(res, gain, shift, w1, b1, w2, b2, we, be, wd, bd, hid):
    K, n = CHUNKS, hid
    rows, D = res.shape[1:]
    FFL, LATL, OUTL = w1.shape[2], we.shape[2], wd.shape[2]
    S = rows // K
    M = n * S
    T = NX = n // 2
    TW = D // n
    dma = pltpu.SemaphoreType.DMA
    vmem = pl.BlockSpec(memory_space=pltpu.VMEM)
    hbm = pl.BlockSpec(memory_space=pl.ANY)
    codes, recon = pl.pallas_call(
        functools.partial(kernel, n),
        out_shape=(
            jax.ShapeDtypeStruct((n * rows, LATL), BF16),
            jax.ShapeDtypeStruct((n * rows, OUTL), F32),
        ),
        in_specs=[vmem] * 7 + [hbm] * 4,
        out_specs=(hbm, hbm),
        scratch_shapes=[
            pltpu.VMEM(w1.shape[1:], BF16),
            pltpu.VMEM(w2.shape[1:], BF16),
            pltpu.VMEM(we.shape[1:], BF16),
            pltpu.VMEM(wd.shape[1:], BF16),
            pltpu.VMEM((K, n, S, D), BF16),
            pltpu.VMEM((M, FFL), BF16),
            pltpu.VMEM((K, T, M, TW), BF16),
            pltpu.VMEM((K, T, M, TW), BF16),
            pltpu.VMEM((K, T, M, TW), F32),
            pltpu.VMEM((K, T, M, TW), BF16),
            pltpu.VMEM((K, T, NX, M, TW), BF16),
            pltpu.VMEM((K, n, M, TW), BF16),
            pltpu.VMEM((K, M, LATL), F32),
            pltpu.VMEM((K, n, S, LATL), BF16),
            pltpu.VMEM((K, n, S, LATL), BF16),
            pltpu.VMEM((K, n, n, S, LATL), BF16),
            pltpu.VMEM((K, M, OUTL), F32),
            dma((4,)),
            dma((K, 2, NX)),
            dma((K, n)),
            dma((K, T)),
            dma((K, T)),
            dma((K, T, NX)),
            dma((K, T, NX)),
            dma((K, T)),
            dma((K, T)),
            dma((K, n)),
            dma((K, n)),
            dma((K, 2, n)),
            dma((K, n)),
            dma((K, n, NX)),
            dma((K, n, NX)),
            dma((K, NX)),
            dma((K, NX)),
            dma((2, K, n)),
        ],
        compiler_params=pltpu.CompilerParams(
            collective_id=0, has_side_effects=True, vmem_limit_bytes=56 * 1024 * 1024
        ),
    )(
        res[0], gain, shift, b1, b2, be.reshape(1, LATL), bd,
        w1[0], w2[0], we[0], wd[0],
    )
    return land(codes, recon[None])


def solution(mesh):
    hid, ckpt = mesh.shape["hid"], mesh.shape["ckpt"]

    def body(*operands):
        rows, width = operands[0].shape[1:]
        latents = operands[7].shape[2]
        fits = hid == ckpt and hid % 2 == 0 and rows % (16 * CHUNKS) == 0
        fits = fits and latents % 256 == 0 and width % (256 * hid) == 0
        return (fused if fits and hid <= 4 else with_collectives)(*operands, **(dict(hid=hid) if fits and hid <= 4 else {}))

    placed = (
        P("ckpt", ("groups", "hid"), None),
        P("ckpt", None),
        P("ckpt", None),
        P("ckpt", None, "hid"),
        P("ckpt", "hid"),
        P("ckpt", "hid", None),
        P("ckpt", None),
        P("ckpt", None, "hid"),
        P("hid"),
        P("ckpt", None, "hid"),
        P("ckpt", "hid"),
    )
    return jax.shard_map(
        body,
        mesh=mesh,
        in_specs=placed,
        out_specs=(P("groups", "hid"), P("ckpt", "groups", "hid")),
        check_vma=False,
    )
```

```python
import functools

import jax
import jax.numpy as jnp
from jax import lax
from jax.experimental import pallas as pl
from jax.experimental.pallas import tpu as pltpu
from jax.sharding import PartitionSpec as P


def with_collectives(
    residual_stream,
    norm_gain,
    norm_shift,
    input_weight,
    input_bias,
    output_weight,
    output_bias,
    encoder_weight,
    encoder_bias,
    decoder_weight,
    decoder_bias,
):
    values = residual_stream[0].astype(jnp.float32)
    average = jnp.mean(values, axis=-1, keepdims=True)
    centred = values - average
    variance = jnp.mean(centred * centred, axis=-1, keepdims=True)
    normed = (centred * lax.rsqrt(variance + 1e-05) * norm_gain[0] + norm_shift[0]).astype(
        jnp.bfloat16
    )
    first_weight = input_weight[0]
    first_bias = input_bias[0]
    second_weight = output_weight[0]
    hidden = jax.nn.gelu(
        jnp.dot(
            lax.all_gather(normed, "hid", axis=0, tiled=True),
            first_weight,
            preferred_element_type=jnp.float32,
        )
        + first_bias,
        approximate=False,
    ).astype(jnp.bfloat16)
    partial_out = jnp.dot(hidden, second_weight, preferred_element_type=jnp.float32)
    mlp_out = (lax.psum(partial_out, "hid") + output_bias[0]).astype(jnp.bfloat16)
    encoder_terms = jnp.dot(mlp_out, encoder_weight[0], preferred_element_type=jnp.float32)
    latent_codes = jax.nn.relu(lax.psum(encoder_terms, "ckpt") + encoder_bias).astype(jnp.bfloat16)
    local_decoder = decoder_weight[0]
    column_count = local_decoder.shape[1]
    rebuilt = (
        jnp.dot(
            lax.all_gather(latent_codes, "hid", axis=1, tiled=True),
            local_decoder,
            preferred_element_type=jnp.float32,
        )
        + decoder_bias[0]
    )
    own_columns = lax.dynamic_slice_in_dim(
        mlp_out, lax.axis_index("hid") * column_count, column_count, 1
    ).astype(jnp.float32)
    recon_error = (own_columns - rebuilt)[None]
    return (latent_codes, recon_error)


CHUNKS = 3
F32, BF16 = jnp.float32, jnp.bfloat16


def kernel(
    n, res, gain, shift, b1, b2, be, bd, w1_hbm, w2_hbm, we_hbm, wd_hbm, codes_out, recon_out,
    w1, w2, we, wd, nbuf, hbuf, psend, precv, pown, xsend, xrecv, mbuf, pre, zsend, zrecv, cbuf, obuf,
    sw, sa, ra, sb, rb, sx, rx, sm, rm, sz, rz, sc, rc, sd, rd, se, re, so,
):
    K = CHUNKS
    S = nbuf.shape[2]
    M = n * S
    D = nbuf.shape[3]
    FFL = w1.shape[1]
    LATL = we.shape[1]
    TW = D // n
    T = n // 2
    NX = n // 2
    NZ = n
    h = lax.axis_index("hid")
    z = lax.axis_index("ckpt")
    c = lax.rem(h, 2)
    sib = h + 1 - 2 * c
    sends = []

    def hpeer(j):
        return lax.rem(h + 2 * j, n)

    def hfrom(j):
        return lax.rem(h + n - 2 * j, n)

    def zpeer(j):
        return lax.rem(z + j, NZ)

    def zfrom(j):
        return lax.rem(z + NZ - j, NZ)

    def remote(src, dst, ssem, rsem, **dev):
        return pltpu.make_async_remote_copy(
            src_ref=src, dst_ref=dst, send_sem=ssem, recv_sem=rsem,
            device_id=dev, device_id_type=pl.DeviceIdType.MESH,
        )

    def send(src, dst, ssem, rsem, **dev):
        copy = remote(src, dst, ssem, rsem, **dev)
        copy.start()
        sends.append(copy)

    def arrived(dst, ssem, rsem):
        remote(dst, dst, ssem, rsem, hid=sib).wait_recv()

    loads = [
        pltpu.make_async_copy(a, b, sw.at[i])
        for i, (a, b) in enumerate(((w1_hbm, w1), (w2_hbm, w2), (we_hbm, we), (wd_hbm, wd)))
    ]
    for load in loads:
        load.start()

    barrier = pltpu.get_barrier_semaphore()
    peers = [dict(hid=sib)] + [dict(hid=hpeer(j)) for j in range(1, NX)]
    peers += [dict(ckpt=zpeer(j)) for j in range(1, NZ)]
    for dev in peers:
        pl.semaphore_signal(barrier, inc=1, device_id=dev, device_id_type=pl.DeviceIdType.MESH)

    def normalise(k):
        values = res[k * S : (k + 1) * S, :].astype(F32)
        average = jnp.mean(values, axis=-1, keepdims=True)
        centred = values - average
        variance = jnp.mean(centred * centred, axis=-1, keepdims=True)
        nbuf[k, h] = (centred * lax.rsqrt(variance + 1e-05) * gain[...] + shift[...]).astype(BF16)

    def spread(k):
        for j in range(1, NX):
            send(nbuf.at[k, h], nbuf.at[k, h], sa.at[k, 1, j], ra.at[k, h], hid=hpeer(j))
        send(nbuf.at[k, h], nbuf.at[k, h], sa.at[k, 0, 0], ra.at[k, h], hid=sib)

    def relay(k):
        for j in range(1, NX):
            o = hfrom(j)
            arrived(nbuf.at[k, o], sa.at[k, 0, 0], ra.at[k, o])
            send(nbuf.at[k, o], nbuf.at[k, o], sa.at[k, 0, j], ra.at[k, o], hid=sib)

    def first(k):
        arrived(nbuf.at[k, sib], sa.at[k, 0, 0], ra.at[k, sib])
        for j in range(1, NX):
            o = lax.rem(sib + n - 2 * j, n)
            arrived(nbuf.at[k, o], sa.at[k, 0, 0], ra.at[k, o])
        if k == 0:
            loads[0].wait()

        def tile(i, _):
            cols = pl.ds(pl.multiple_of(i * 256, 256), 256)
            u = jnp.dot(nbuf[k].reshape(M, D), w1[:, cols], preferred_element_type=F32) + b1[:, cols]
            hbuf[:, cols] = (0.5 * u * (1.0 + lax.erf(u * 0.7071067811865476))).astype(BF16)
            return 0

        lax.fori_loop(0, FFL // 256, tile, 0)

    def project(g):
        cols = pl.ds(pl.multiple_of(g * TW, TW), TW)
        return jnp.dot(hbuf[...], w2[:, cols], preferred_element_type=F32)

    def second(k, between):
        if k == 0:
            loads[1].wait()
        for t in range(T):
            psend[k, t] = project((1 - c) * T + t).astype(BF16)
            send(psend.at[k, t], precv.at[k, t], sb.at[k, t], rb.at[k, t], hid=sib)
        between()
        for t in range(T):
            own = project(c * T + t)
            arrived(precv.at[k, t], sb.at[k, t], rb.at[k, t])
            own = own + precv[k, t].astype(F32)
            pown[k, t] = own
            xsend[k, t] = own.astype(BF16)
            for j in range(1, NX):
                send(xsend.at[k, t], xrecv.at[k, t, j], sx.at[k, t, j], rx.at[k, t, j], hid=hpeer(j))

    def encode(k, g, start):
        rows = pl.ds(pl.multiple_of(g * TW, TW), TW)

        def tile(i, _):
            cols = pl.ds(pl.multiple_of(i * 256, 256), 256)
            u = jnp.dot(mbuf[k, g], we[rows, cols], preferred_element_type=F32)
            pre[k, :, cols] = u if start else pre[k, :, cols] + u
            return 0

        lax.fori_loop(0, LATL // 256, tile, 0)

    def finish(k):
        for t in range(T):
            g = c * T + t
            total = pown[k, t]
            for j in range(1, NX):
                arrived(xrecv.at[k, t, j], sx.at[k, t, j], rx.at[k, t, j])
                total = total + xrecv[k, t, j].astype(F32)
            mbuf[k, g] = (total + b2[:, pl.ds(pl.multiple_of(g * TW, TW), TW)]).astype(BF16)
            send(mbuf.at[k, g], mbuf.at[k, g], sm.at[k, t], rm.at[k, t], hid=sib)
            if k == 0 and t == 0:
                loads[2].wait()
            encode(k, g, t == 0)
        for t in range(T):
            g = (1 - c) * T + t
            arrived(mbuf.at[k, g], sm.at[k, t], rm.at[k, t])
            encode(k, g, False)
        for j in range(1, NZ):
            b = zpeer(j)
            zsend[k, j] = pre[k, pl.ds(pl.multiple_of(b * S, S), S), :].astype(BF16)
            send(zsend.at[k, j], zrecv.at[k, j], sz.at[k, j], rz.at[k, j], ckpt=b)

    def codes(k):
        total = pre[k, pl.ds(pl.multiple_of(z * S, S), S), :]
        for j in range(1, NZ):
            arrived(zrecv.at[k, j], sz.at[k, j], rz.at[k, j])
            total = total + zrecv[k, j].astype(F32)
        cbuf[k, h, z] = jnp.maximum(total + be[...], 0.0).astype(BF16)
        pl.when(z < NZ - 1)(passing(k, z, 1).start)
        pl.when(z > 0)(passing(k, z, 0).start)
        over(k, z)

    def passing(k, b, up):
        there = jnp.minimum(z + 1, NZ - 1) if up else jnp.maximum(z - 1, 0)
        block = cbuf.at[k, h, b]
        return remote(block, block, sc.at[k, up, b], rc.at[k, b], ckpt=there)

    def over(k, b):
        for j in range(1, NX):
            crossing(k, b, j).start()

    def crossing(k, b, j):
        block = cbuf.at[k, h, b]
        return remote(block, block, sd.at[k, b, j], rd.at[k, b, j], hid=hpeer(j))

    def passed():
        for k in range(K):
            for b in range(NZ):
                pl.when(jnp.logical_and(b <= z, z < NZ - 1))(passing(k, b, 1).wait_send)
                pl.when(jnp.logical_and(b >= z, z > 0))(passing(k, b, 0).wait_send)
                for j in range(1, NX):
                    crossing(k, b, j).wait_send()

    outs = []

    def put(src, dst, sem):
        copy = pltpu.make_async_copy(src, dst, sem)
        copy.start()
        outs.append(copy)

    def collect(k):
        for i in range(1, NZ):
            @pl.when(z - i >= 0)
            def _():
                b = z - i
                arrived(cbuf.at[k, h, b], sc.at[k, 0, b], rc.at[k, b])
                pl.when(z < NZ - 1)(passing(k, b, 1).start)
                over(k, b)

            @pl.when(z + i < NZ)
            def _():
                b = z + i
                arrived(cbuf.at[k, h, b], sc.at[k, 0, b], rc.at[k, b])
                pl.when(z > 0)(passing(k, b, 0).start)
                over(k, b)

        send(cbuf.at[k, h], cbuf.at[k, h], se.at[k, 0], re.at[k, 0], hid=sib)
        for b in range(NZ):
            put(cbuf.at[k, h, b], codes_out.at[pl.ds((b * K + k) * S, S), :], so.at[0, k, b])

    def decode(k):
        def part(o):
            return jnp.dot(
                cbuf[k, o].reshape(M, LATL),
                wd[pl.ds(pl.multiple_of(o * LATL, LATL), LATL), :],
                preferred_element_type=F32,
            )

        if k == 0:
            loads[3].wait()
        obuf[k] = mbuf[k, h].astype(F32) - (part(h) + bd[...])
        arrived(cbuf.at[k, sib], se.at[k, 0], re.at[k, 0])
        obuf[k] -= part(sib)
        for j in range(1, NX):
            o = hfrom(j)
            for b in range(NZ):
                arrived(cbuf.at[k, o, b], sd.at[k, b, j], rd.at[k, b, j])
            send(cbuf.at[k, o], cbuf.at[k, o], se.at[k, j], re.at[k, j], hid=sib)
            obuf[k] -= part(o)
        for j in range(1, NX):
            o = lax.rem(sib + n - 2 * j, n)
            arrived(cbuf.at[k, o], se.at[k, j], re.at[k, j])
            obuf[k] -= part(o)
        for b in range(NZ):
            put(obuf.at[k, pl.ds(b * S, S), :], recon_out.at[pl.ds((b * K + k) * S, S), :], so.at[1, k, b])

    normalise(0)
    pl.semaphore_wait(barrier, len(peers))
    spread(0)
    for k in range(1, K):
        normalise(k)
        spread(k)
    def later(k):
        second(k, functools.partial(relay, k + 1) if k + 1 < K else (lambda: None))

    relay(0)
    first(0)
    later(0)
    first(1)
    later(1)
    first(2)
    finish(0)
    later(2)
    finish(1)
    codes(0)
    finish(2)
    codes(1)
    collect(0)
    codes(2)
    collect(1)
    decode(0)
    collect(2)
    decode(1)
    decode(2)
    for copy in outs:
        copy.wait()
    for copy in sends:
        copy.wait_send()
    passed()


def landing(codes, recon, codes_out, recon_out):
    codes_out[...] = codes[...]
    recon_out[...] = recon[...]


def land(codes, recon):
    vmem = pl.BlockSpec(memory_space=pltpu.VMEM)
    return pl.pallas_call(
        landing,
        out_shape=(
            jax.ShapeDtypeStruct(codes.shape, codes.dtype),
            jax.ShapeDtypeStruct(recon.shape, recon.dtype),
        ),
        in_specs=[vmem] * 2,
        out_specs=(vmem, vmem),
    )(codes, recon)


def fused(res, gain, shift, w1, b1, w2, b2, we, be, wd, bd, hid):
    K, n = CHUNKS, hid
    rows, D = res.shape[1:]
    FFL, LATL, OUTL = w1.shape[2], we.shape[2], wd.shape[2]
    S = rows // K
    M = n * S
    T = NX = n // 2
    TW = D // n
    dma = pltpu.SemaphoreType.DMA
    vmem = pl.BlockSpec(memory_space=pltpu.VMEM)
    hbm = pl.BlockSpec(memory_space=pl.ANY)
    codes, recon = pl.pallas_call(
        functools.partial(kernel, n),
        out_shape=(
            jax.ShapeDtypeStruct((n * rows, LATL), BF16),
            jax.ShapeDtypeStruct((n * rows, OUTL), F32),
        ),
        in_specs=[vmem] * 7 + [hbm] * 4,
        out_specs=(hbm, hbm),
        scratch_shapes=[
            pltpu.VMEM(w1.shape[1:], BF16),
            pltpu.VMEM(w2.shape[1:], BF16),
            pltpu.VMEM(we.shape[1:], BF16),
            pltpu.VMEM(wd.shape[1:], BF16),
            pltpu.VMEM((K, n, S, D), BF16),
            pltpu.VMEM((M, FFL), BF16),
            pltpu.VMEM((K, T, M, TW), BF16),
            pltpu.VMEM((K, T, M, TW), BF16),
            pltpu.VMEM((K, T, M, TW), F32),
            pltpu.VMEM((K, T, M, TW), BF16),
            pltpu.VMEM((K, T, NX, M, TW), BF16),
            pltpu.VMEM((K, n, M, TW), BF16),
            pltpu.VMEM((K, M, LATL), F32),
            pltpu.VMEM((K, n, S, LATL), BF16),
            pltpu.VMEM((K, n, S, LATL), BF16),
            pltpu.VMEM((K, n, n, S, LATL), BF16),
            pltpu.VMEM((K, M, OUTL), F32),
            dma((4,)),
            dma((K, 2, NX)),
            dma((K, n)),
            dma((K, T)),
            dma((K, T)),
            dma((K, T, NX)),
            dma((K, T, NX)),
            dma((K, T)),
            dma((K, T)),
            dma((K, n)),
            dma((K, n)),
            dma((K, 2, n)),
            dma((K, n)),
            dma((K, n, NX)),
            dma((K, n, NX)),
            dma((K, NX)),
            dma((K, NX)),
            dma((2, K, n)),
        ],
        compiler_params=pltpu.CompilerParams(
            collective_id=0, has_side_effects=True, vmem_limit_bytes=56 * 1024 * 1024
        ),
    )(
        res[0], gain, shift, b1, b2, be.reshape(1, LATL), bd,
        w1[0], w2[0], we[0], wd[0],
    )
    return land(codes, recon[None])


def solution(mesh):
    hid, ckpt = mesh.shape["hid"], mesh.shape["ckpt"]

    def body(*operands):
        rows, width = operands[0].shape[1:]
        latents = operands[7].shape[2]
        fits = hid == ckpt and hid % 2 == 0 and rows % (16 * CHUNKS) == 0
        fits = fits and latents % 256 == 0 and width % (256 * hid) == 0
        return (fused if fits and hid <= 4 else with_collectives)(*operands, **(dict(hid=hid) if fits and hid <= 4 else {}))

    placed = (
        P("ckpt", ("groups", "hid"), None),
        P("ckpt", None),
        P("ckpt", None),
        P("ckpt", None, "hid"),
        P("ckpt", "hid"),
        P("ckpt", "hid", None),
        P("ckpt", None),
        P("ckpt", None, "hid"),
        P("hid"),
        P("ckpt", None, "hid"),
        P("ckpt", "hid"),
    )
    return jax.shard_map(
        body,
        mesh=mesh,
        in_specs=placed,
        out_specs=(P("groups", "hid"), P("ckpt", "groups", "hid")),
        check_vma=False,
    )
```
